32 devices in a mesh: groups: 2 (over x), ctx: 16 (over z, y, core).
Axes of the slice: x: 2, y: 2, z: 4, core: 2. Of those that a mesh axis runs over, the one named last changes fastest.
Arguments:
- queries: bfloat16 [6144, 2048], P(('groups', 'ctx')), parts along dimension 0, may hold values from -6 to 6
- patch_keys: bfloat16 [6144, 512], P(('groups', 'ctx')), parts along dimension 0, may hold values from -6 to 6
- patch_values: bfloat16 [6144, 512], P(('groups', 'ctx')), parts along dimension 0, may hold values from -6 to 6
- patch_counts: int32 [32], P('groups'), parts along dimension 0, may hold values from 64 to 192, as said below
Outputs:
- attended: bfloat16 [6144, 2048], P(('groups', 'ctx')), parts along dimension 0
The draws below stay inside these ranges and needn't reach their ends.
There are 2 independent parts, one for each index of `groups`. The reference program is written for one: setup_inputs(seed, part) draws one part's arguments, and reference() takes and returns one part's arrays. A program takes and returns all parts, laid end to end along the dimension named above; each array names one. Nothing has to cross between parts.
Inputs may be any that keep to these rules, and one draw needn't show every extreme that they name: patch_counts[i] patches fill slots 0 to patch_counts[i] - 1 of shard i; the counts sum to 2048, and starts[i] differs from i * 128 by at most a quarter of 128.
All inputs are finite; a program needn't handle non-finite values.
Results may differ from the reference program's by a relative error of at most 0.0044.
Values may be sent and summed in bfloat16 or wider, within the bound.
A program may use at most 192 MiB of HBM per device.

```python
import jax
import jax.numpy as jnp
from jax import lax

Q_HEADS = 16
KV_HEADS = 4
HEAD_DIM = 128
GROUP = 4
P_DEV = 128
CAP = 192
TOTAL = 2048
N_CTX = 16


def draw_queries(key, part):
    key = jax.random.fold_in(key, 11)
    row_count = N_CTX * CAP
    entries = jnp.clip(jax.random.normal(key, (row_count, Q_HEADS * HEAD_DIM), jnp.float32), -6.0, 6.0)
    return entries.astype(jnp.bfloat16)


def draw_patch_keys(key, part):
    key = jax.random.fold_in(key, 23)
    row_count = N_CTX * CAP
    entries = jnp.clip(jax.random.normal(key, (row_count, KV_HEADS * HEAD_DIM), jnp.float32), -6.0, 6.0)
    return entries.astype(jnp.bfloat16)


def draw_patch_counts(key, part):
    key = jax.random.fold_in(key, 5)
    first_key, second_key = jax.random.split(key)
    quarter = P_DEV // 4
    surplus = jax.random.randint(first_key, (N_CTX,), -quarter, quarter + 1, dtype=jnp.int32)
    chosen_at = jax.random.randint(second_key, (), 1, N_CTX - 2, dtype=jnp.int32)
    device_ids = jnp.arange(N_CTX, dtype=jnp.int32)
    surplus = jnp.where(device_ids == chosen_at - 1, -quarter, surplus)
    surplus = jnp.where(device_ids == chosen_at, quarter, surplus)
    surplus = jnp.where(device_ids == chosen_at + 1, -quarter, surplus)
    surplus = jnp.where(device_ids == N_CTX - 1, 0, surplus)
    before = jnp.concatenate([jnp.zeros((1,), jnp.int32), surplus[:-1]])
    return (P_DEV + surplus - before).astype(jnp.int32)


def levels(key, dims, cuts, least, high):
    factor_of, own = 1.0, jax.random.fold_in(key, 6)
    for axis_at, parts in cuts:
        steps = jnp.exp(jax.random.uniform(jax.random.fold_in(own, axis_at), (parts,), jnp.float32, least / len(cuts), high / len(cuts)))
        factor_of = factor_of * jnp.repeat(steps, dims[axis_at] // parts).reshape([-1 if axis == axis_at else 1 for axis in range(len(dims))])
    return factor_of


def gaussian(rng, dims, scale, most, cuts=(), held_as=jnp.bfloat16):
    loudness = levels(rng, dims, cuts, -0.22, 0.18) if cuts else 1.0
    values = jax.random.normal(rng, dims, jnp.float32) * scale * loudness
    return jnp.minimum(jnp.maximum(values, -most), most).astype(held_as)


def setup_inputs(seed: int = 0, part: int = 0) -> dict:
    key_of = jax.random.split(jax.random.key(seed), 5)
    own_keys = jax.random.split(jax.random.fold_in(key_of[4], part), 5)
    queries = draw_queries(jax.random.fold_in(jax.random.fold_in(key_of[4], part), 71), part)
    patch_keys = draw_patch_keys(jax.random.fold_in(jax.random.fold_in(key_of[4], part), 71), part)
    patch_values = gaussian(own_keys[2], (N_CTX * CAP, KV_HEADS * HEAD_DIM), 1.0, 6.0, ((0, 16),))
    patch_counts = draw_patch_counts(jax.random.fold_in(jax.random.fold_in(key_of[4], part), 71), part)
    return {"queries": queries, "patch_keys": patch_keys, "patch_values": patch_values, "patch_counts": patch_counts}


masked_score = -1e30


def reference(queries, patch_keys, patch_values, patch_counts):
    counts_int = patch_counts.astype(jnp.int32)
    starts = (jnp.cumsum(counts_int).astype(jnp.int32) - counts_int).astype(jnp.int32)
    slot_order = jnp.arange(CAP, dtype=jnp.int32)
    positions = (starts[:, None] + slot_order[None, :]).reshape(-1).astype(jnp.int32)
    filled = (slot_order[None, :] < counts_int[:, None]).reshape(-1)
    target = jnp.where(filled, positions, TOTAL).astype(jnp.int32)
    kv_width = KV_HEADS * HEAD_DIM
    key_rows = jnp.zeros((TOTAL, kv_width), jnp.float32).at[target].set(patch_keys.astype(jnp.float32), mode="drop")
    value_rows = jnp.zeros((TOTAL, kv_width), jnp.float32).at[target].set(patch_values.astype(jnp.float32), mode="drop")
    key_heads = key_rows.reshape(TOTAL, KV_HEADS, HEAD_DIM)
    value_heads = value_rows.reshape(TOTAL, KV_HEADS, HEAD_DIM)
    key_order = jnp.arange(TOTAL, dtype=jnp.int32)
    score_scale = HEAD_DIM ** -0.5

    def one_shard(pieces):
        shard_rows, shard_place, shard_live = pieces
        grouped = shard_rows.astype(jnp.float32).reshape(CAP, KV_HEADS, GROUP, HEAD_DIM)
        scores = jnp.einsum("rkgd,mkd->kgrm", grouped, key_heads) * score_scale
        visible = key_order[None, :] <= shard_place[:, None]
        scores = jnp.where(visible, scores, masked_score)
        highest = jnp.max(scores, axis=-1, keepdims=True)
        weights = jnp.exp(scores - highest)
        weight_sum = jnp.sum(weights, axis=-1)
        rounded = lax.optimization_barrier(weights.astype(jnp.bfloat16))
        blended = jnp.einsum("kgrm,mkd->kgrd", rounded.astype(jnp.float32), value_heads)
        blended = blended / weight_sum[..., None]
        result = blended.transpose(2, 0, 1, 3).reshape(CAP, Q_HEADS * HEAD_DIM)
        return jnp.where(shard_live[:, None], result, 0.0).astype(jnp.bfloat16)

    shaped = queries.reshape(N_CTX, CAP, Q_HEADS * HEAD_DIM)
    result = lax.map(one_shard, (shaped, positions.reshape(N_CTX, CAP), filled.reshape(N_CTX, CAP)))
    return result.reshape(N_CTX * CAP, Q_HEADS * HEAD_DIM)
```

```python
import functools

import jax
import jax.numpy as jnp
from jax import lax
from jax.experimental import pallas as pl
from jax.experimental.pallas import tpu as pltpu
from jax.sharding import PartitionSpec as P

KV_HEADS = 4
GROUP = 4
HEAD_DIM = 128
HIDDEN = -1e30
LOG2E = 1.4426950408889634
EXPONENT_SCALE = LOG2E * HEAD_DIM ** (-0.5)
MESH = pl.DeviceIdType.MESH

FAR_PLACE = 2**20


def kernel(
    ranks,
    q_ref,
    k_ref,
    v_ref,
    counts_ref,
    out_ref,
    near,
    far,
    beside,
    mine,
    edge_out,
    edge_in,
    stacked,
    total,
    highest,
    weight_sum,
    own_send,
    near_send,
    far_send,
    beside_recv,
    near_recv,
    far_recv,
    edge_send,
    edge_recv,
):
    slots = q_ref.shape[0]
    mean = mine.shape[1]
    quarter = edge_in.shape[2]
    planes = ranks // 4
    part_index = lax.axis_index("groups")
    rank = lax.axis_index("ctx")
    plane, row, side = rank // 4, (rank // 2) % 2, rank % 2
    mate = rank + 1 - 2 * side
    over = rank + 2 - 4 * row

    partners = (
        (mate, None),
        (over, None),
        (rank - 1, (side == 0) & (rank > 0)),
        (rank + 1, (side == 1) & (rank < ranks - 1)),
        (rank - 4, plane > 0),
        (rank + 4, plane < planes - 1),
    )
    barrier = pltpu.get_barrier_semaphore()
    expected = 0
    for partner, there in partners:
        if there is None:
            pl.semaphore_signal(barrier, inc=1, device_id=(part_index, partner), device_id_type=MESH)
            expected = expected + 1
        else:

            @pl.when(there)
            def _(partner=partner):
                pl.semaphore_signal(barrier, inc=1, device_id=(part_index, partner), device_id_type=MESH)

            expected = expected + there.astype(jnp.int32)

    own_start = lax.fori_loop(
        0, ranks, lambda j, s: s + jnp.where(j < rank, counts_ref[j], 0), jnp.int32(0)
    )
    own_count = counts_ref[rank]

    place = lax.broadcasted_iota(jnp.int32, (slots, slots), 0) + (mean * rank - quarter - own_start)
    slot = lax.broadcasted_iota(jnp.int32, (slots, slots), 1)
    pick = jnp.where((place == slot) & (slot < own_count), 1.0, 0.0).astype(jnp.bfloat16)
    for part, ref in enumerate((k_ref, v_ref)):
        placed = jnp.dot(pick, ref[...], preferred_element_type=jnp.float32).astype(jnp.bfloat16)
        half = slice(part * HEAD_DIM, (part + 1) * HEAD_DIM)
        for head in range(KV_HEADS):
            rows = placed[:, head * HEAD_DIM : (head + 1) * HEAD_DIM]
            edge_out[0, head, :, half] = rows[:quarter]
            mine[head, :, half] = rows[quarter : quarter + mean]
            edge_out[1, head, :, half] = rows[quarter + mean :]

    pl.semaphore_wait(barrier, expected)

    def edge(which):
        return pltpu.make_async_remote_copy(
            src_ref=edge_out.at[which],
            dst_ref=edge_in.at[which],
            send_sem=edge_send.at[which],
            recv_sem=edge_recv.at[which],
            device_id=(part_index, (rank + 2 * which - 1 + ranks) % ranks),
            device_id_type=MESH,
        )

    first, last = rank == 0, rank == ranks - 1

    @pl.when(jnp.logical_not(first))
    def _():
        edge(0).start()

    @pl.when(jnp.logical_not(last))
    def _():
        edge(1).start()

    def head_columns(head):
        return pl.ds(pl.multiple_of(head * HEAD_DIM, HEAD_DIM), HEAD_DIM)

    def scores_of(keys, head):
        return lax.dot_general(
            keys, stacked[head], (((1,), (1,)), ((), ())), preferred_element_type=jnp.float32
        )

    def blend(values, weights):
        return lax.dot_general(
            values,
            weights.astype(jnp.bfloat16),
            (((0,), (0,)), ((), ())),
            preferred_element_type=jnp.float32,
        )

    lanes = GROUP * slots

    def own(head, _):
        for g in range(GROUP):
            column = pl.multiple_of((head * GROUP + g) * HEAD_DIM, HEAD_DIM)
            stacked[head, g * slots : (g + 1) * slots, :] = q_ref[:, pl.ds(column, HEAD_DIM)]
        scores = scores_of(k_ref[:, head_columns(head)], head)
        key_slot = lax.broadcasted_iota(jnp.int32, (slots, lanes), 0)
        query_slot = lax.broadcasted_iota(jnp.int32, (slots, lanes), 1) % slots
        scores = jnp.where(key_slot <= query_slot, scores, HIDDEN)
        top = jnp.max(scores, axis=0, keepdims=True)
        weights = jnp.exp2((scores - top) * EXPONENT_SCALE)
        highest[head] = top
        weight_sum[head] = jnp.sum(weights, axis=0, keepdims=True)
        total[head] = blend(v_ref[:, head_columns(head)], weights)
        return 0

    lax.fori_loop(0, KV_HEADS, own, 0)

    def absorb(head, rows, visible):
        scores = scores_of(rows[:, :HEAD_DIM], head)
        if visible is not None:
            scores = jnp.where(visible, scores, HIDDEN)
        before = highest[head]
        top = jnp.maximum(before, jnp.max(scores, axis=0, keepdims=True))
        rescale = jnp.exp2((before - top) * EXPONENT_SCALE)
        weights = jnp.exp2((scores - top) * EXPONENT_SCALE)
        highest[head] = top
        weight_sum[head] = weight_sum[head] * rescale + jnp.sum(weights, axis=0, keepdims=True)
        total[head] = total[head] * rescale + blend(rows[:, HEAD_DIM:], weights)

    def before_own(first_place, count):
        return lax.broadcasted_iota(jnp.int32, (count, lanes), 0) + first_place < own_start

    def absorb_pair(pair, mask):
        def one(head, _):
            rows = jnp.concatenate([pair[0, head], pair[1, head]])
            visible = None
            if mask is not None:
                visible = jnp.concatenate(
                    [
                        jnp.full((mean, lanes), True),
                        before_own(jnp.where(mask, mean * (rank - 1), -FAR_PLACE), mean),
                    ]
                )
            absorb(head, rows, visible)
            return 0

        lax.fori_loop(0, KV_HEADS, one, 0)

    def copy(source, landing, send_sem, recv_sem, target):
        return pltpu.make_async_remote_copy(
            src_ref=source,
            dst_ref=landing,
            send_sem=send_sem,
            recv_sem=recv_sem,
            device_id=(part_index, target),
            device_id_type=MESH,
        )

    more = plane < planes - 1

    def own_copies():
        return (
            (row == 0, copy(mine, far[0].at[0], own_send.at[1], far_recv.at[0, 0], over)),
            (more, copy(mine, near[0].at[0], own_send.at[0], near_recv.at[0, 0], rank + 4))
            if planes > 1
            else (None, None),
            (side == 0, copy(mine, beside, own_send.at[2], beside_recv, mate)),
        )

    def near_copies(s):
        here = near[s].at[0]
        along = (None, None)
        if s + 1 < planes - 1:
            landing = near[s + 1].at[0]
            along = (
                more,
                copy(here, landing, near_send.at[s, 0], near_recv.at[s + 1, 0], rank + 4),
            )
        return (
            along,
            (True, copy(here, far[s + 1].at[0], near_send.at[s, 1], far_recv.at[s + 1, 0], over)),
            (True, copy(here, near[s].at[1], near_send.at[s, 2], near_recv.at[s, 1], mate)),
        )

    def far_copies(s):
        return (
            (True, copy(far[s].at[0], far[s].at[1], far_send.at[s], far_recv.at[s, 1], mate)),
        )

    def each(copies, act):
        for wanted, item in copies:
            if wanted is True:
                act(item)
            elif wanted is not None:

                @pl.when(wanted)
                def _(item=item):
                    act(item)

    def start(item):
        item.start()

    def finish(item):
        item.wait_send()

    def arrived(landing, recv_sem):
        copy(landing, landing, own_send.at[0], recv_sem, mate).wait_recv()

    @pl.when(jnp.logical_not(first))
    def _():
        edge(1).wait_recv()
        mine[:, :quarter] = mine[:, :quarter] + edge_in[1]

    @pl.when(jnp.logical_not(last))
    def _():
        edge(0).wait_recv()
        mine[:, mean - quarter :] = mine[:, mean - quarter :] + edge_in[0]

    each(own_copies(), start)

    @pl.when(jnp.logical_not(first))
    def _():
        def tail(head, _):
            absorb(head, edge_in[1, head], before_own(mean * rank, quarter))
            return 0

        lax.fori_loop(0, KV_HEADS, tail, 0)

    @pl.when(side == 1)
    def _():
        arrived(beside, beside_recv)

        def before(head, _):
            absorb(head, beside[head], before_own(mean * mate, mean))
            return 0

        lax.fori_loop(0, KV_HEADS, before, 0)

    for s in range(planes):
        with_near = s < plane
        with_far = row == 1 if s == 0 else s <= plane

        if s < planes - 1:

            @pl.when(with_near)
            def _(s=s):
                arrived(near[s].at[0], near_recv.at[s, 0])
                each(near_copies(s), start)

        @pl.when(with_far)
        def _(s=s):
            arrived(far[s].at[0], far_recv.at[s, 0])
            each(far_copies(s), start)

        if s < planes - 1:

            @pl.when(with_near)
            def _(s=s):
                arrived(near[s].at[1], near_recv.at[s, 1])
                absorb_pair(near[s], None)

        @pl.when(with_far)
        def _(s=s):
            arrived(far[s].at[1], far_recv.at[s, 1])
            follows = (side == 0) & (row == 1 - s)
            absorb_pair(far[s], follows if s < 2 else None)

    alive = lax.broadcasted_iota(jnp.int32, (slots, HEAD_DIM), 0) < own_count

    def write(head, _):
        result = (total[head] / weight_sum[head]).T
        for g in range(GROUP):
            column = pl.multiple_of((head * GROUP + g) * HEAD_DIM, HEAD_DIM)
            piece = jnp.where(alive, result[g * slots : (g + 1) * slots], 0.0)
            out_ref[:, pl.ds(column, HEAD_DIM)] = piece.astype(jnp.bfloat16)
        return 0

    lax.fori_loop(0, KV_HEADS, write, 0)

    @pl.when(jnp.logical_not(first))
    def _():
        edge(0).wait_send()

    @pl.when(jnp.logical_not(last))
    def _():
        edge(1).wait_send()

    each(own_copies(), finish)
    for s in range(planes):
        if s < planes - 1:

            @pl.when(s < plane)
            def _(s=s):
                each(near_copies(s), finish)

        @pl.when(row == 1 if s == 0 else s <= plane)
        def _(s=s):
            each(far_copies(s), finish)


def per_device(ranks, queries, patch_keys, patch_values, patch_counts):
    slots = patch_keys.shape[0]
    mean = slots * 2 // 3
    quarter = mean // 4
    lanes = GROUP * slots
    planes = ranks // 4
    return pl.pallas_call(
        functools.partial(kernel, ranks),
        out_shape=jax.ShapeDtypeStruct(queries.shape, jnp.bfloat16),
        in_specs=[pl.BlockSpec(memory_space=pltpu.VMEM)] * 3
        + [pl.BlockSpec(memory_space=pltpu.SMEM)],
        out_specs=pl.BlockSpec(memory_space=pltpu.VMEM),
        scratch_shapes=[
            [pltpu.VMEM((2, KV_HEADS, mean, 2 * HEAD_DIM), jnp.bfloat16)] * (planes - 1),
            [pltpu.VMEM((2, KV_HEADS, mean, 2 * HEAD_DIM), jnp.bfloat16)] * planes,
            pltpu.VMEM((KV_HEADS, mean, 2 * HEAD_DIM), jnp.bfloat16),
            pltpu.VMEM((KV_HEADS, mean, 2 * HEAD_DIM), jnp.bfloat16),
            pltpu.VMEM((2, KV_HEADS, quarter, 2 * HEAD_DIM), jnp.bfloat16),
            pltpu.VMEM((2, KV_HEADS, quarter, 2 * HEAD_DIM), jnp.bfloat16),
            pltpu.VMEM((KV_HEADS, lanes, HEAD_DIM), jnp.bfloat16),
            pltpu.VMEM((KV_HEADS, HEAD_DIM, lanes), jnp.float32),
            pltpu.VMEM((KV_HEADS, 1, lanes), jnp.float32),
            pltpu.VMEM((KV_HEADS, 1, lanes), jnp.float32),
            pltpu.SemaphoreType.DMA((3,)),
            pltpu.SemaphoreType.DMA((planes, 3)),
            pltpu.SemaphoreType.DMA((planes,)),
            pltpu.SemaphoreType.DMA,
            pltpu.SemaphoreType.DMA((planes, 2)),
            pltpu.SemaphoreType.DMA((planes, 2)),
            pltpu.SemaphoreType.DMA((2,)),
            pltpu.SemaphoreType.DMA((2,)),
        ],
        compiler_params=pltpu.CompilerParams(
            collective_id=0, has_side_effects=True, vmem_limit_bytes=52 * 2**20
        ),
    )(queries, patch_keys, patch_values, patch_counts)


def solution(mesh):
    placed = (
        P(("groups", "ctx"), None),
        P(("groups", "ctx"), None),
        P(("groups", "ctx"), None),
        P("groups"),
    )
    return jax.shard_map(
        functools.partial(per_device, mesh.shape["ctx"]),
        mesh=mesh,
        in_specs=placed,
        out_specs=P(("groups", "ctx"), None),
        check_vma=False,
    )
```

```python
import functools

import jax
import jax.numpy as jnp
from jax import lax
from jax.experimental import pallas as pl
from jax.experimental.pallas import tpu as pltpu
from jax.sharding import PartitionSpec as P

KV_HEADS = 4
GROUP = 4
HEAD_DIM = 128
HIDDEN = -1e30
LOG2E = 1.4426950408889634
EXPONENT_SCALE = LOG2E * HEAD_DIM ** (-0.5)
MESH = pl.DeviceIdType.MESH

FAR_PLACE = 2**20


def kernel(
    ranks,
    q_hbm,
    k_hbm,
    v_hbm,
    counts_ref,
    out_ref,
    k_ref,
    v_ref,
    near,
    far,
    beside,
    mine,
    edge_out,
    edge_in,
    stacked,
    total,
    highest,
    weight_sum,
    load_sems,
    query_sems,
    own_send,
    near_send,
    far_send,
    beside_recv,
    near_recv,
    far_recv,
    edge_send,
    edge_recv,
):
    slots = k_ref.shape[0]
    quarter = edge_in.shape[2]
    mean = 4 * quarter
    planes = ranks // 4
    lanes = GROUP * slots
    part_index = lax.axis_index("groups")
    rank = lax.axis_index("ctx")
    plane, row, side = rank // 4, (rank // 2) % 2, rank % 2
    mate = rank + 1 - 2 * side
    over = rank + 2 - 4 * row
    first, last = rank == 0, rank == ranks - 1

    partners = (
        (mate, None),
        (over, None),
        (rank - 1, (side == 0) & (rank > 0)),
        (rank + 1, (side == 1) & (rank < ranks - 1)),
        (rank - 4, plane > 0),
        (rank + 4, plane < planes - 1),
    )
    barrier = pltpu.get_barrier_semaphore()
    expected = 0
    for partner, there in partners:
        if there is None:
            pl.semaphore_signal(
                barrier, inc=1, device_id=(part_index, partner), device_id_type=MESH
            )
            expected = expected + 1
        else:

            @pl.when(there)
            def _(partner=partner):
                pl.semaphore_signal(
                    barrier, inc=1, device_id=(part_index, partner), device_id_type=MESH
                )

            expected = expected + there.astype(jnp.int32)

    loads = (
        pltpu.make_async_copy(k_hbm, k_ref, load_sems.at[0]),
        pltpu.make_async_copy(v_hbm, v_ref, load_sems.at[1]),
    )
    for load in loads:
        load.start()
    query_loads = [
        pltpu.make_async_copy(
            q_hbm.at[:, pl.ds((head * GROUP + g) * HEAD_DIM, HEAD_DIM)],
            stacked.at[head, pl.ds(g * slots, slots)],
            query_sems.at[head * GROUP + g],
        )
        for head in range(KV_HEADS)
        for g in range(GROUP)
    ]
    for load in query_loads:
        load.start()

    own_start = lax.fori_loop(
        0, ranks, lambda j, s: s + jnp.where(j < rank, counts_ref[j], 0), jnp.int32(0)
    )
    own_count = counts_ref[rank]

    place = lax.broadcasted_iota(jnp.int32, (slots, slots), 0) + (mean * rank - quarter - own_start)
    slot = lax.broadcasted_iota(jnp.int32, (slots, slots), 1)
    pick = jnp.where((place == slot) & (slot < own_count), 1.0, 0.0).astype(jnp.bfloat16)
    for part, ref in enumerate((k_ref, v_ref)):
        loads[part].wait()
        placed = jnp.dot(pick, ref[...], preferred_element_type=jnp.float32).astype(jnp.bfloat16)
        half = slice(part * HEAD_DIM, (part + 1) * HEAD_DIM)
        for head in range(KV_HEADS):
            rows = placed[:, head * HEAD_DIM : (head + 1) * HEAD_DIM]
            edge_out[0, head, :, half] = rows[:quarter]
            mine[1, head, :quarter, half] = rows[quarter : 2 * quarter]
            mine[0, head, :, half] = rows[2 * quarter : 4 * quarter]
            mine[1, head, quarter:, half] = rows[4 * quarter : 5 * quarter]
            edge_out[1, head, :, half] = rows[5 * quarter :]

    @pl.when(first)
    def _():
        edge_in[1] = jnp.zeros(edge_in.shape[1:], edge_in.dtype)

    pl.semaphore_wait(barrier, expected)

    def copy(source, landing, send_sem, recv_sem, target):
        return pltpu.make_async_remote_copy(
            src_ref=source,
            dst_ref=landing,
            send_sem=send_sem,
            recv_sem=recv_sem,
            device_id=(part_index, target),
            device_id_type=MESH,
        )

    def edge(which):
        return copy(
            edge_out.at[which],
            edge_in.at[which],
            edge_send.at[which],
            edge_recv.at[which],
            (rank + 2 * which - 1 + ranks) % ranks,
        )

    more = plane < planes - 1

    def own_copies(p):
        source = mine.at[p]
        along = (None, None)
        if planes > 1:
            along = (
                more,
                copy(source, near[0].at[0, p], own_send.at[p, 0], near_recv.at[0, 0, p], rank + 4),
            )
        return (
            (row == 0, copy(source, far[0].at[0, p], own_send.at[p, 1], far_recv.at[0, 0, p], over)),
            along,
            (side == 0, copy(source, beside.at[p], own_send.at[p, 2], beside_recv.at[p], mate)),
        )

    def near_copies(s, p):
        source = near[s].at[0, p]
        along = (None, None)
        if s + 1 < planes - 1:
            along = (
                more,
                copy(
                    source,
                    near[s + 1].at[0, p],
                    near_send.at[s, p, 0],
                    near_recv.at[s + 1, 0, p],
                    rank + 4,
                ),
            )
        return (
            along,
            (
                True,
                copy(
                    source,
                    far[s + 1].at[0, p],
                    near_send.at[s, p, 1],
                    far_recv.at[s + 1, 0, p],
                    over,
                ),
            ),
            (
                True,
                copy(source, near[s].at[1, p], near_send.at[s, p, 2], near_recv.at[s, 1, p], mate),
            ),
        )

    def far_copies(s, p):
        return (
            (
                True,
                copy(far[s].at[0, p], far[s].at[1, p], far_send.at[s, p], far_recv.at[s, 1, p], mate),
            ),
        )

    def each(copies, act):
        for wanted, item in copies:
            if wanted is True:
                act(item)
            elif wanted is not None:

                @pl.when(wanted)
                def _(item=item):
                    act(item)

    def start(item):
        item.start()

    def finish(item):
        item.wait_send()

    def arrived(landing, recv_sem):
        copy(landing, landing, own_send.at[0, 0], recv_sem, mate).wait_recv()

    @pl.when(jnp.logical_not(first))
    def _():
        edge(0).start()

    @pl.when(jnp.logical_not(last))
    def _():
        edge(1).start()

    each(own_copies(0), start)

    for load in query_loads:
        load.wait()

    @pl.when(jnp.logical_not(first))
    def _():
        edge(1).wait_recv()
        mine[1, :, :quarter] = mine[1, :, :quarter] + edge_in[1]

    @pl.when(jnp.logical_not(last))
    def _():
        edge(0).wait_recv()
        mine[1, :, quarter:] = mine[1, :, quarter:] + edge_in[0]

    each(own_copies(1), start)

    def each_head(act):
        if planes <= 4:
            for head in range(KV_HEADS):
                act(head)
        else:

            def one(head, _):
                act(head)
                return 0

            lax.fori_loop(0, KV_HEADS, one, 0)

    def scores_of(keys, head):
        return lax.dot_general(
            keys, stacked[head], (((1,), (1,)), ((), ())), preferred_element_type=jnp.float32
        )

    def blend(values, weights):
        return lax.dot_general(
            values,
            weights.astype(jnp.bfloat16),
            (((0,), (0,)), ((), ())),
            preferred_element_type=jnp.float32,
        )

    def head_columns(head):
        return pl.ds(pl.multiple_of(head * HEAD_DIM, HEAD_DIM), HEAD_DIM)

    def before_own(first_place):
        at = lax.broadcasted_iota(jnp.int32, (quarter, lanes), 0) + first_place
        return at < own_start

    def own(head):
        tail = edge_in[1, head]
        keys = jnp.concatenate([k_ref[:, head_columns(head)], tail[:, :HEAD_DIM]])
        values = jnp.concatenate([v_ref[:, head_columns(head)], tail[:, HEAD_DIM:]])
        scores = scores_of(keys, head)
        key_slot = lax.broadcasted_iota(jnp.int32, (slots, lanes), 0)
        query_slot = lax.broadcasted_iota(jnp.int32, (slots, lanes), 1) % slots
        scores = jnp.concatenate(
            [
                jnp.where(key_slot <= query_slot, scores[:slots], HIDDEN),
                jnp.where(before_own(mean * rank), scores[slots:], HIDDEN),
            ]
        )
        top = jnp.max(scores, axis=0, keepdims=True)
        weights = jnp.exp2((scores - top) * EXPONENT_SCALE)
        highest[head] = top
        weight_sum[head] = jnp.sum(weights, axis=0, keepdims=True)
        total[head] = blend(values, weights)

    def absorb(head, rows, visible):
        scores = scores_of(rows[:, :HEAD_DIM], head)
        if visible is not None:
            scores = jnp.concatenate(
                [scores[:-quarter], jnp.where(visible, scores[-quarter:], HIDDEN)]
            )
        before = highest[head]
        top = jnp.maximum(before, jnp.max(scores, axis=0, keepdims=True))
        rescale = jnp.exp2((before - top) * EXPONENT_SCALE)
        weights = jnp.exp2((scores - top) * EXPONENT_SCALE)
        highest[head] = top
        weight_sum[head] = weight_sum[head] * rescale + jnp.sum(weights, axis=0, keepdims=True)
        total[head] = total[head] * rescale + blend(rows[:, HEAD_DIM:], weights)

    def absorb_pair(pair, follows):
        visible = None
        if follows is not None:
            visible = before_own(jnp.where(follows, mean * rank - quarter, -FAR_PLACE))

        def one(head):
            rows = jnp.concatenate([pair[i, p, head] for i in (0, 1) for p in (0, 1)])
            absorb(head, rows, visible)

        each_head(one)

    each_head(own)

    @pl.when(side == 1)
    def _():
        for p in (0, 1):
            arrived(beside.at[p], beside_recv.at[p])
        visible = before_own(mean * rank - quarter)

        def one(head):
            absorb(head, jnp.concatenate([beside[p, head] for p in (0, 1)]), visible)

        each_head(one)

    for s in range(planes):
        with_near = s < plane
        with_far = row == 1 if s == 0 else s <= plane

        for p in (0, 1):
            if s < planes - 1:

                @pl.when(with_near)
                def _(s=s, p=p):
                    arrived(near[s].at[0, p], near_recv.at[s, 0, p])
                    each(near_copies(s, p), start)

            @pl.when(with_far)
            def _(s=s, p=p):
                arrived(far[s].at[0, p], far_recv.at[s, 0, p])
                each(far_copies(s, p), start)

        if s < planes - 1:

            @pl.when(with_near)
            def _(s=s):
                for p in (0, 1):
                    arrived(near[s].at[1, p], near_recv.at[s, 1, p])
                absorb_pair(near[s], None)

        @pl.when(with_far)
        def _(s=s):
            for p in (0, 1):
                arrived(far[s].at[1, p], far_recv.at[s, 1, p])
            absorb_pair(far[s], (side == 0) & (row == 1 - s) if s < 2 else None)

    alive = lax.broadcasted_iota(jnp.int32, (slots, HEAD_DIM), 0) < own_count

    def write(head):
        result = (total[head] / weight_sum[head]).T
        for g in range(GROUP):
            column = pl.multiple_of((head * GROUP + g) * HEAD_DIM, HEAD_DIM)
            piece = jnp.where(alive, result[g * slots : (g + 1) * slots], 0.0)
            out_ref[:, pl.ds(column, HEAD_DIM)] = piece.astype(jnp.bfloat16)

    each_head(write)

    @pl.when(jnp.logical_not(first))
    def _():
        edge(0).wait_send()

    @pl.when(jnp.logical_not(last))
    def _():
        edge(1).wait_send()

    for p in (0, 1):
        each(own_copies(p), finish)
        for s in range(planes):
            if s < planes - 1:

                @pl.when(s < plane)
                def _(s=s, p=p):
                    each(near_copies(s, p), finish)

            @pl.when(row == 1 if s == 0 else s <= plane)
            def _(s=s, p=p):
                each(far_copies(s, p), finish)


def per_device(ranks, queries, patch_keys, patch_values, patch_counts):
    slots, width = patch_keys.shape
    quarter = slots // 6
    lanes = GROUP * slots
    planes = ranks // 4
    two_parts = (2, KV_HEADS, 2 * quarter, 2 * HEAD_DIM)
    pair = pltpu.VMEM((2, *two_parts), jnp.bfloat16)
    edges = pltpu.VMEM((2, KV_HEADS, quarter, 2 * HEAD_DIM), jnp.bfloat16)
    return pl.pallas_call(
        functools.partial(kernel, ranks),
        out_shape=jax.ShapeDtypeStruct(queries.shape, jnp.bfloat16),
        in_specs=[pl.BlockSpec(memory_space=pl.ANY)] * 3
        + [pl.BlockSpec(memory_space=pltpu.SMEM)],
        out_specs=pl.BlockSpec(memory_space=pltpu.VMEM),
        scratch_shapes=[
            pltpu.VMEM((slots, width), jnp.bfloat16),
            pltpu.VMEM((slots, width), jnp.bfloat16),
            [pair] * (planes - 1),
            [pair] * planes,
            pltpu.VMEM(two_parts, jnp.bfloat16),
            pltpu.VMEM(two_parts, jnp.bfloat16),
            edges,
            edges,
            pltpu.VMEM((KV_HEADS, lanes, HEAD_DIM), jnp.bfloat16),
            pltpu.VMEM((KV_HEADS, HEAD_DIM, lanes), jnp.float32),
            pltpu.VMEM((KV_HEADS, 1, lanes), jnp.float32),
            pltpu.VMEM((KV_HEADS, 1, lanes), jnp.float32),
            pltpu.SemaphoreType.DMA((2,)),
            pltpu.SemaphoreType.DMA((KV_HEADS * GROUP,)),
            pltpu.SemaphoreType.DMA((2, 3)),
            pltpu.SemaphoreType.DMA((planes, 2, 3)),
            pltpu.SemaphoreType.DMA((planes, 2)),
            pltpu.SemaphoreType.DMA((2,)),
            pltpu.SemaphoreType.DMA((planes, 2, 2)),
            pltpu.SemaphoreType.DMA((planes, 2, 2)),
            pltpu.SemaphoreType.DMA((2,)),
            pltpu.SemaphoreType.DMA((2,)),
        ],
        compiler_params=pltpu.CompilerParams(
            collective_id=0, has_side_effects=True, vmem_limit_bytes=60 * 2**20
        ),
    )(queries, patch_keys, patch_values, patch_counts)


def solution(mesh):
    placed = (
        P(("groups", "ctx"), None),
        P(("groups", "ctx"), None),
        P(("groups", "ctx"), None),
        P("groups"),
    )
    return jax.shard_map(
        functools.partial(per_device, mesh.shape["ctx"]),
        mesh=mesh,
        in_specs=placed,
        out_specs=P(("groups", "ctx"), None),
        check_vma=False,
    )
```

```python
import functools

import jax
import jax.numpy as jnp
from jax import lax
from jax.experimental import pallas as pl
from jax.experimental.pallas import tpu as pltpu
from jax.sharding import PartitionSpec as P

KV_HEADS = 4
GROUP = 4
HEAD_DIM = 128
HIDDEN = -1e30
LOG2E = 1.4426950408889634
EXPONENT_SCALE = LOG2E * HEAD_DIM ** (-0.5)
MESH = pl.DeviceIdType.MESH

FAR_PLACE = 2**20


def kernel(
    ranks,
    q_hbm,
    k_hbm,
    v_hbm,
    counts_hbm,
    out_ref,
    counts_ref,
    k_ref,
    v_ref,
    near,
    far,
    beside,
    mine,
    edge_out,
    edge_in,
    stacked,
    turned,
    total,
    highest,
    weight_sum,
    load_sems,
    query_sems,
    own_send,
    near_send,
    far_send,
    beside_recv,
    near_recv,
    far_recv,
    edge_send,
    edge_recv,
):
    slots = k_ref.shape[0]
    quarter = edge_in.shape[2]
    mean = 4 * quarter
    planes = ranks // 4
    lanes = GROUP * slots
    part_index = lax.axis_index("groups")
    rank = lax.axis_index("ctx")
    plane, row, side = rank // 4, (rank // 2) % 2, rank % 2
    mate = rank + 1 - 2 * side
    over = rank + 2 - 4 * row
    first, last = rank == 0, rank == ranks - 1

    partners = (
        (mate, None),
        (over, None),
        (rank - 1, (side == 0) & (rank > 0)),
        (rank + 1, (side == 1) & (rank < ranks - 1)),
        (rank - 4, plane > 0),
        (rank + 4, plane < planes - 1),
    )
    barrier = pltpu.get_barrier_semaphore()
    expected = 0
    for partner, there in partners:
        if there is None:
            pl.semaphore_signal(
                barrier, inc=1, device_id=(part_index, partner), device_id_type=MESH
            )
            expected = expected + 1
        else:

            @pl.when(there)
            def _(partner=partner):
                pl.semaphore_signal(
                    barrier, inc=1, device_id=(part_index, partner), device_id_type=MESH
                )

            expected = expected + there.astype(jnp.int32)

    loads = (
        pltpu.make_async_copy(k_hbm, k_ref, load_sems.at[0]),
        pltpu.make_async_copy(v_hbm, v_ref, load_sems.at[1]),
        pltpu.make_async_copy(counts_hbm, counts_ref, load_sems.at[2]),
    )
    for load in loads:
        load.start()
    query_loads = [
        pltpu.make_async_copy(
            q_hbm.at[:, pl.ds((head * GROUP + g) * HEAD_DIM, HEAD_DIM)],
            stacked.at[head, pl.ds(g * slots, slots)],
            query_sems.at[head * GROUP + g],
        )
        for head in range(KV_HEADS)
        for g in range(GROUP)
    ]
    for load in query_loads:
        load.start()

    loads[2].wait()
    own_start = lax.fori_loop(
        0, ranks, lambda j, s: s + jnp.where(j < rank, counts_ref[j], 0), jnp.int32(0)
    )
    own_count = counts_ref[rank]

    place = lax.broadcasted_iota(jnp.int32, (slots, slots), 0) + (mean * rank - quarter - own_start)
    slot = lax.broadcasted_iota(jnp.int32, (slots, slots), 1)
    pick = jnp.where((place == slot) & (slot < own_count), 1.0, 0.0).astype(jnp.bfloat16)
    for part, ref in enumerate((k_ref, v_ref)):
        loads[part].wait()
        placed = jnp.dot(pick, ref[...], preferred_element_type=jnp.float32).astype(jnp.bfloat16)
        half = slice(part * HEAD_DIM, (part + 1) * HEAD_DIM)
        for head in range(KV_HEADS):
            rows = placed[:, head * HEAD_DIM : (head + 1) * HEAD_DIM]
            edge_out[0, head, :, half] = rows[:quarter]
            mine[1, head, :quarter, half] = rows[quarter : 2 * quarter]
            mine[0, head, :, half] = rows[2 * quarter : 4 * quarter]
            mine[1, head, quarter:, half] = rows[4 * quarter : 5 * quarter]
            edge_out[1, head, :, half] = rows[5 * quarter :]

    @pl.when(first)
    def _():
        edge_in[1] = jnp.zeros(edge_in.shape[1:], edge_in.dtype)

    pl.semaphore_wait(barrier, expected)

    def copy(source, landing, send_sem, recv_sem, target):
        return pltpu.make_async_remote_copy(
            src_ref=source,
            dst_ref=landing,
            send_sem=send_sem,
            recv_sem=recv_sem,
            device_id=(part_index, target),
            device_id_type=MESH,
        )

    def edge(which):
        return copy(
            edge_out.at[which],
            edge_in.at[which],
            edge_send.at[which],
            edge_recv.at[which],
            (rank + 2 * which - 1 + ranks) % ranks,
        )

    more = plane < planes - 1

    def own_copies(p):
        source = mine.at[p]
        along = (None, None)
        if planes > 1:
            along = (
                more,
                copy(source, near[0].at[0, p], own_send.at[p, 0], near_recv.at[0, 0, p], rank + 4),
            )
        return (
            (row == 0, copy(source, far[0].at[0, p], own_send.at[p, 1], far_recv.at[0, 0, p], over)),
            along,
            (side == 0, copy(source, beside.at[p], own_send.at[p, 2], beside_recv.at[p], mate)),
        )

    def near_copies(s, p):
        source = near[s].at[0, p]
        along = (None, None)
        if s + 1 < planes - 1:
            along = (
                more,
                copy(
                    source,
                    near[s + 1].at[0, p],
                    near_send.at[s, p, 0],
                    near_recv.at[s + 1, 0, p],
                    rank + 4,
                ),
            )
        return (
            along,
            (
                True,
                copy(
                    source,
                    far[s + 1].at[0, p],
                    near_send.at[s, p, 1],
                    far_recv.at[s + 1, 0, p],
                    over,
                ),
            ),
            (
                True,
                copy(source, near[s].at[1, p], near_send.at[s, p, 2], near_recv.at[s, 1, p], mate),
            ),
        )

    def far_copies(s, p):
        source = far[s].at[0, p]
        return (
            (True, copy(source, far[s].at[1, p], far_send.at[s, p], far_recv.at[s, 1, p], mate)),
        )

    def each(copies, act):
        for wanted, item in copies:
            if wanted is True:
                act(item)
            elif wanted is not None:

                @pl.when(wanted)
                def _(item=item):
                    act(item)

    def start(item):
        item.start()

    def finish(item):
        item.wait_send()

    def arrived(landing, recv_sem):
        copy(landing, landing, own_send.at[0, 0], recv_sem, mate).wait_recv()

    @pl.when(jnp.logical_not(first))
    def _():
        edge(0).start()

    @pl.when(jnp.logical_not(last))
    def _():
        edge(1).start()

    each(own_copies(0), start)

    for load in query_loads:
        load.wait()
    for head in range(KV_HEADS):
        turned[head] = stacked[head].T

    @pl.when(jnp.logical_not(first))
    def _():
        edge(1).wait_recv()
        mine[1, :, :quarter] = mine[1, :, :quarter] + edge_in[1]

    @pl.when(jnp.logical_not(last))
    def _():
        edge(0).wait_recv()
        mine[1, :, quarter:] = mine[1, :, quarter:] + edge_in[0]

    each(own_copies(1), start)

    def each_head(act):
        if planes <= 4:
            for head in range(KV_HEADS):
                act(head)
        else:

            def one(head, _):
                act(head)
                return 0

            lax.fori_loop(0, KV_HEADS, one, 0)

    def scores_of(keys, head):
        return lax.dot_general(
            keys, turned[head], (((1,), (0,)), ((), ())), preferred_element_type=jnp.float32
        )

    def blend(values, weights):
        return lax.dot_general(
            values,
            weights.astype(jnp.bfloat16),
            (((0,), (0,)), ((), ())),
            preferred_element_type=jnp.float32,
        )

    def head_columns(head):
        return pl.ds(pl.multiple_of(head * HEAD_DIM, HEAD_DIM), HEAD_DIM)

    def before_own(first_place):
        at = lax.broadcasted_iota(jnp.int32, (quarter, lanes), 0) + first_place
        return at < own_start

    def own(head):
        tail = edge_in[1, head]
        keys = jnp.concatenate([k_ref[:, head_columns(head)], tail[:, :HEAD_DIM]])
        values = jnp.concatenate([v_ref[:, head_columns(head)], tail[:, HEAD_DIM:]])
        scores = scores_of(keys, head)
        key_slot = lax.broadcasted_iota(jnp.int32, (slots, lanes), 0)
        query_slot = lax.broadcasted_iota(jnp.int32, (slots, lanes), 1) % slots
        scores = jnp.concatenate(
            [
                jnp.where(key_slot <= query_slot, scores[:slots], HIDDEN),
                jnp.where(before_own(mean * rank), scores[slots:], HIDDEN),
            ]
        )
        top = jnp.max(scores, axis=0, keepdims=True)
        weights = jnp.exp2((scores - top) * EXPONENT_SCALE)
        highest[head] = top
        weight_sum[head] = jnp.sum(weights, axis=0, keepdims=True)
        total[head] = blend(values, weights)

    def absorb_all(rows_of, visible):
        def score(head):
            rows = rows_of(head)
            scores = scores_of(rows[:, :HEAD_DIM], head)
            if visible is not None:
                scores = jnp.concatenate(
                    [scores[:-quarter], jnp.where(visible, scores[-quarter:], HIDDEN)]
                )
            return scores, rows[:, HEAD_DIM:]

        def weigh(head, scores):
            before = highest[head]
            top = jnp.maximum(before, jnp.max(scores, axis=0, keepdims=True))
            rescale = jnp.exp2((before - top) * EXPONENT_SCALE)
            weights = jnp.exp2((scores - top) * EXPONENT_SCALE)
            highest[head] = top
            weight_sum[head] = weight_sum[head] * rescale + jnp.sum(weights, axis=0, keepdims=True)
            return rescale, weights.astype(jnp.bfloat16)

        def gather(head, rescale, weights, values):
            total[head] = total[head] * rescale + blend(values, weights)

        if planes > 4:

            def one(head, _):
                scores, values = score(head)
                gather(head, *weigh(head, scores), values)
                return 0

            lax.fori_loop(0, KV_HEADS, one, 0)
            return
        held = [score(head) for head in range(KV_HEADS)]
        weighed = [weigh(head, held[head][0]) for head in range(KV_HEADS)]
        for head in range(KV_HEADS):
            gather(head, *weighed[head], held[head][1])

    def absorb_pair(pair, follows):
        visible = None
        if follows is not None:
            visible = before_own(jnp.where(follows, mean * rank - quarter, -FAR_PLACE))

        absorb_all(
            lambda head: jnp.concatenate([pair[i, p, head] for i in (0, 1) for p in (0, 1)]), visible
        )

    def near_step(s):
        @pl.when(s < plane)
        def _():
            for p in (0, 1):
                arrived(near[s].at[1, p], near_recv.at[s, 1, p])
            absorb_pair(near[s], None)

    def far_step(s, when):
        @pl.when(when)
        def _():
            for p in (0, 1):
                arrived(far[s].at[1, p], far_recv.at[s, 1, p])
            absorb_pair(far[s], (side == 0) & (row == 1 - s) if s < 2 else None)

    for s in range(planes):
        with_far = row == 1 if s == 0 else s <= plane
        for p in (0, 1):
            if s < planes - 1:

                @pl.when(s < plane)
                def _(s=s, p=p):
                    arrived(near[s].at[0, p], near_recv.at[s, 0, p])
                    each(near_copies(s, p), start)

            @pl.when(with_far)
            def _(s=s, p=p):
                arrived(far[s].at[0, p], far_recv.at[s, 0, p])
                each(far_copies(s, p), start)

            if p == 0 and s == 0:
                each_head(own)
            elif p == 0:
                near_step(s - 1)
                far_step(s - 1, (s <= plane) & ((row == 1) if s == 1 else True))
        if s == 0:

            @pl.when(side == 1)
            def _():
                for p in (0, 1):
                    arrived(beside.at[p], beside_recv.at[p])
                visible = before_own(mean * rank - quarter)
                absorb_all(lambda head: jnp.concatenate([beside[p, head] for p in (0, 1)]), visible)

        far_step(s, (s == plane) & ((row == 1) if s == 0 else True))

    alive = lax.broadcasted_iota(jnp.int32, (slots, HEAD_DIM), 0) < own_count

    def write(head):
        result = (total[head] / weight_sum[head]).T
        for g in range(GROUP):
            column = pl.multiple_of((head * GROUP + g) * HEAD_DIM, HEAD_DIM)
            piece = jnp.where(alive, result[g * slots : (g + 1) * slots], 0.0)
            out_ref[:, pl.ds(column, HEAD_DIM)] = piece.astype(jnp.bfloat16)

    each_head(write)

    @pl.when(jnp.logical_not(first))
    def _():
        edge(0).wait_send()

    @pl.when(jnp.logical_not(last))
    def _():
        edge(1).wait_send()

    for p in (0, 1):
        each(own_copies(p), finish)
        for s in range(planes):
            if s < planes - 1:

                @pl.when(s < plane)
                def _(s=s, p=p):
                    each(near_copies(s, p), finish)

            @pl.when(row == 1 if s == 0 else s <= plane)
            def _(s=s, p=p):
                each(far_copies(s, p), finish)


def per_device(ranks, queries, patch_keys, patch_values, patch_counts):
    slots, width = patch_keys.shape
    quarter = slots // 6
    lanes = GROUP * slots
    planes = ranks // 4
    two_parts = (2, KV_HEADS, 2 * quarter, 2 * HEAD_DIM)
    pair = pltpu.VMEM((2, *two_parts), jnp.bfloat16)
    edges = pltpu.VMEM((2, KV_HEADS, quarter, 2 * HEAD_DIM), jnp.bfloat16)
    return pl.pallas_call(
        functools.partial(kernel, ranks),
        out_shape=jax.ShapeDtypeStruct(queries.shape, jnp.bfloat16),
        in_specs=[pl.BlockSpec(memory_space=pl.ANY)] * 4,
        out_specs=pl.BlockSpec(memory_space=pltpu.VMEM),
        scratch_shapes=[
            pltpu.SMEM(patch_counts.shape, jnp.int32),
            pltpu.VMEM((slots, width), jnp.bfloat16),
            pltpu.VMEM((slots, width), jnp.bfloat16),
            [pair] * (planes - 1),
            [pair] * planes,
            pltpu.VMEM(two_parts, jnp.bfloat16),
            pltpu.VMEM(two_parts, jnp.bfloat16),
            edges,
            edges,
            pltpu.VMEM((KV_HEADS, lanes, HEAD_DIM), jnp.bfloat16),
            pltpu.VMEM((KV_HEADS, HEAD_DIM, lanes), jnp.bfloat16),
            pltpu.VMEM((KV_HEADS, HEAD_DIM, lanes), jnp.float32),
            pltpu.VMEM((KV_HEADS, 1, lanes), jnp.float32),
            pltpu.VMEM((KV_HEADS, 1, lanes), jnp.float32),
            pltpu.SemaphoreType.DMA((3,)),
            pltpu.SemaphoreType.DMA((KV_HEADS * GROUP,)),
            pltpu.SemaphoreType.DMA((2, 3)),
            pltpu.SemaphoreType.DMA((planes, 2, 3)),
            pltpu.SemaphoreType.DMA((planes, 2)),
            pltpu.SemaphoreType.DMA((2,)),
            pltpu.SemaphoreType.DMA((planes, 2, 2)),
            pltpu.SemaphoreType.DMA((planes, 2, 2)),
            pltpu.SemaphoreType.DMA((2,)),
            pltpu.SemaphoreType.DMA((2,)),
        ],
        compiler_params=pltpu.CompilerParams(
            collective_id=0, has_side_effects=True, vmem_limit_bytes=60 * 2**20
        ),
    )(queries, patch_keys, patch_values, patch_counts)


def solution(mesh):
    placed = (
        P(("groups", "ctx"), None),
        P(("groups", "ctx"), None),
        P(("groups", "ctx"), None),
        P("groups"),
    )
    return jax.shard_map(
        functools.partial(per_device, mesh.shape["ctx"]),
        mesh=mesh,
        in_specs=placed,
        out_specs=P(("groups", "ctx"), None),
        check_vma=False,
    )
```

```python
import functools

import jax
import jax.numpy as jnp
from jax import lax
from jax.experimental import pallas as pl
from jax.experimental.pallas import tpu as pltpu
from jax.sharding import PartitionSpec as P

KV_HEADS = 4
GROUP = 4
HEAD_DIM = 128
HIDDEN = -1e30
LOG2E = 1.4426950408889634
EXPONENT_SCALE = LOG2E * HEAD_DIM ** (-0.5)
MESH = pl.DeviceIdType.MESH

FAR_PLACE = 2**20


def kernel(
    ranks,
    q_hbm,
    k_hbm,
    v_hbm,
    counts_hbm,
    out_ref,
    counts_ref,
    k_ref,
    v_ref,
    near,
    far,
    beside,
    mine,
    edge_out,
    edge_in,
    stacked,
    turned,
    total,
    highest,
    weight_sum,
    load_sems,
    query_sems,
    own_send,
    near_send,
    far_send,
    beside_recv,
    near_recv,
    far_recv,
    edge_send,
    edge_recv,
):
    slots = k_ref.shape[0]
    quarter = edge_in.shape[2]
    mean = 4 * quarter
    planes = ranks // 4
    lanes = GROUP * slots
    part_index = lax.axis_index("groups")
    rank = lax.axis_index("ctx")
    plane, row, side = rank // 4, (rank // 2) % 2, rank % 2
    mate = rank + 1 - 2 * side
    over = rank + 2 - 4 * row
    first, last = rank == 0, rank == ranks - 1

    partners = (
        (mate, None),
        (over, None),
        (rank - 1, (side == 0) & (rank > 0)),
        (rank + 1, (side == 1) & (rank < ranks - 1)),
        (rank - 4, plane > 0),
        (rank + 4, plane < planes - 1),
    )
    barrier = pltpu.get_barrier_semaphore()
    expected = 0
    for partner, there in partners:
        if there is None:
            pl.semaphore_signal(
                barrier, inc=1, device_id=(part_index, partner), device_id_type=MESH
            )
            expected = expected + 1
        else:

            @pl.when(there)
            def _(partner=partner):
                pl.semaphore_signal(
                    barrier, inc=1, device_id=(part_index, partner), device_id_type=MESH
                )

            expected = expected + there.astype(jnp.int32)

    loads = (
        pltpu.make_async_copy(k_hbm, k_ref, load_sems.at[0]),
        pltpu.make_async_copy(v_hbm, v_ref, load_sems.at[1]),
        pltpu.make_async_copy(counts_hbm, counts_ref, load_sems.at[2]),
    )
    for load in loads:
        load.start()
    query_loads = [
        pltpu.make_async_copy(
            q_hbm.at[:, pl.ds((head * GROUP + g) * HEAD_DIM, HEAD_DIM)],
            stacked.at[head, pl.ds(g * slots, slots)],
            query_sems.at[head * GROUP + g],
        )
        for head in range(KV_HEADS)
        for g in range(GROUP)
    ]
    for load in query_loads:
        load.start()

    loads[2].wait()
    own_start = lax.fori_loop(
        0, ranks, lambda j, s: s + jnp.where(j < rank, counts_ref[j], 0), jnp.int32(0)
    )
    own_count = counts_ref[rank]

    place = lax.broadcasted_iota(jnp.int32, (slots, slots), 0) + (mean * rank - quarter - own_start)
    slot = lax.broadcasted_iota(jnp.int32, (slots, slots), 1)
    pick = jnp.where((place == slot) & (slot < own_count), 1.0, 0.0).astype(jnp.bfloat16)
    for part, ref in enumerate((k_ref, v_ref)):
        loads[part].wait()
        placed = jnp.dot(pick, ref[...], preferred_element_type=jnp.float32).astype(jnp.bfloat16)
        half = slice(part * HEAD_DIM, (part + 1) * HEAD_DIM)
        for head in range(KV_HEADS):
            rows = placed[:, head * HEAD_DIM : (head + 1) * HEAD_DIM]
            edge_out[0, head, :, half] = rows[:quarter]
            mine[1, head, :quarter, half] = rows[quarter : 2 * quarter]
            mine[0, head, :, half] = rows[2 * quarter : 4 * quarter]
            mine[1, head, quarter:, half] = rows[4 * quarter : 5 * quarter]
            edge_out[1, head, :, half] = rows[5 * quarter :]

    @pl.when(first)
    def _():
        edge_in[1] = jnp.zeros(edge_in.shape[1:], edge_in.dtype)

    pl.semaphore_wait(barrier, expected)

    def copy(source, landing, send_sem, recv_sem, target):
        return pltpu.make_async_remote_copy(
            src_ref=source,
            dst_ref=landing,
            send_sem=send_sem,
            recv_sem=recv_sem,
            device_id=(part_index, target),
            device_id_type=MESH,
        )

    def edge(which):
        return copy(
            edge_out.at[which],
            edge_in.at[which],
            edge_send.at[which],
            edge_recv.at[which],
            (rank + 2 * which - 1 + ranks) % ranks,
        )

    more = plane < planes - 1

    def own_copies(p):
        source = mine.at[p]
        along = (None, None)
        if planes > 1:
            along = (
                more,
                copy(source, near[0].at[0, p], own_send.at[p, 0], near_recv.at[0, 0, p], rank + 4),
            )
        return (
            (row == 0, copy(source, far[0].at[0, p], own_send.at[p, 1], far_recv.at[0, 0, p], over)),
            along,
            (side == 0, copy(source, beside.at[p], own_send.at[p, 2], beside_recv.at[p], mate)),
        )

    def near_copies(s, p):
        source = near[s].at[0, p]
        along = (None, None)
        if s + 1 < planes - 1:
            along = (
                more,
                copy(
                    source,
                    near[s + 1].at[0, p],
                    near_send.at[s, p, 0],
                    near_recv.at[s + 1, 0, p],
                    rank + 4,
                ),
            )
        return (
            along,
            (
                True,
                copy(
                    source,
                    far[s + 1].at[0, p],
                    near_send.at[s, p, 1],
                    far_recv.at[s + 1, 0, p],
                    over,
                ),
            ),
            (
                True,
                copy(source, near[s].at[1, p], near_send.at[s, p, 2], near_recv.at[s, 1, p], mate),
            ),
        )

    def far_copies(s, p):
        source = far[s].at[0, p]
        return (
            (True, copy(source, far[s].at[1, p], far_send.at[s, p], far_recv.at[s, 1, p], mate)),
        )

    def each(copies, act):
        for wanted, item in copies:
            if wanted is True:
                act(item)
            elif wanted is not None:

                @pl.when(wanted)
                def _(item=item):
                    act(item)

    def start(item):
        item.start()

    def finish(item):
        item.wait_send()

    def arrived(landing, recv_sem):
        copy(landing, landing, own_send.at[0, 0], recv_sem, mate).wait_recv()

    @pl.when(jnp.logical_not(first))
    def _():
        edge(0).start()

    @pl.when(jnp.logical_not(last))
    def _():
        edge(1).start()

    each(own_copies(0), start)

    for load in query_loads:
        load.wait()
    for head in range(KV_HEADS):
        turned[head] = stacked[head].T

    @pl.when(jnp.logical_not(first))
    def _():
        edge(1).wait_recv()
        mine[1, :, :quarter] = mine[1, :, :quarter] + edge_in[1]

    @pl.when(jnp.logical_not(last))
    def _():
        edge(0).wait_recv()
        mine[1, :, quarter:] = mine[1, :, quarter:] + edge_in[0]

    each(own_copies(1), start)

    def each_head(act):
        if planes <= 4:
            for head in range(KV_HEADS):
                act(head)
        else:

            def one(head, _):
                act(head)
                return 0

            lax.fori_loop(0, KV_HEADS, one, 0)

    def scores_of(keys, head):
        return lax.dot_general(
            keys, turned[head], (((1,), (0,)), ((), ())), preferred_element_type=jnp.float32
        )

    def blend(values, weights):
        return lax.dot_general(
            values,
            weights.astype(jnp.bfloat16),
            (((0,), (0,)), ((), ())),
            preferred_element_type=jnp.float32,
        )

    def head_columns(head):
        return pl.ds(pl.multiple_of(head * HEAD_DIM, HEAD_DIM), HEAD_DIM)

    def before_own(first_place):
        at = lax.broadcasted_iota(jnp.int32, (quarter, lanes), 0) + first_place
        return at < own_start

    def own(head):
        tail = edge_in[1, head]
        keys = jnp.concatenate([k_ref[:, head_columns(head)], tail[:, :HEAD_DIM]])
        values = jnp.concatenate([v_ref[:, head_columns(head)], tail[:, HEAD_DIM:]])
        scores = scores_of(keys, head)
        key_slot = lax.broadcasted_iota(jnp.int32, (slots, lanes), 0)
        query_slot = lax.broadcasted_iota(jnp.int32, (slots, lanes), 1) % slots
        scores = jnp.concatenate(
            [
                jnp.where(key_slot <= query_slot, scores[:slots], HIDDEN),
                jnp.where(before_own(mean * rank), scores[slots:], HIDDEN),
            ]
        )
        top = jnp.max(scores, axis=0, keepdims=True)
        weights = jnp.exp2((scores - top) * EXPONENT_SCALE)
        highest[head] = top
        weight_sum[head] = jnp.sum(weights, axis=0, keepdims=True)
        total[head] = blend(values, weights)

    def absorb_all(rows_of, visible):
        def score(head):
            rows = rows_of(head)
            scores = scores_of(rows[:, :HEAD_DIM], head)
            if visible is not None:
                scores = jnp.concatenate(
                    [scores[:-quarter], jnp.where(visible, scores[-quarter:], HIDDEN)]
                )
            return scores, rows[:, HEAD_DIM:]

        def weigh(head, scores):
            before = highest[head]
            top = jnp.maximum(before, jnp.max(scores, axis=0, keepdims=True))
            rescale = jnp.exp2((before - top) * EXPONENT_SCALE)
            weights = jnp.exp2((scores - top) * EXPONENT_SCALE)
            highest[head] = top
            weight_sum[head] = weight_sum[head] * rescale + jnp.sum(weights, axis=0, keepdims=True)
            return rescale, weights.astype(jnp.bfloat16)

        def gather(head, rescale, weights, values):
            total[head] = total[head] * rescale + blend(values, weights)

        if planes > 4:

            def one(head, _):
                scores, values = score(head)
                gather(head, *weigh(head, scores), values)
                return 0

            lax.fori_loop(0, KV_HEADS, one, 0)
            return
        held = [score(head) for head in range(KV_HEADS)]
        weighed = [weigh(head, held[head][0]) for head in range(KV_HEADS)]
        for head in range(KV_HEADS):
            gather(head, *weighed[head], held[head][1])

    def absorb_pair(pair, follows):
        visible = None
        if follows is not None:
            visible = before_own(jnp.where(follows, mean * rank - quarter, -FAR_PLACE))

        absorb_all(
            lambda head: jnp.concatenate([pair[i, p, head] for i in (0, 1) for p in (0, 1)]), visible
        )

    def near_step(s):
        @pl.when(s < plane)
        def _():
            for p in (0, 1):
                arrived(near[s].at[1, p], near_recv.at[s, 1, p])
            absorb_pair(near[s], None)

    def far_step(s, when):
        @pl.when(when)
        def _():
            for p in (0, 1):
                arrived(far[s].at[1, p], far_recv.at[s, 1, p])
            absorb_pair(far[s], (side == 0) & (row == 1 - s) if s < 2 else None)

    for s in range(planes):
        with_far = row == 1 if s == 0 else s <= plane
        for p in (0, 1):
            if s < planes - 1:

                @pl.when(s < plane)
                def _(s=s, p=p):
                    arrived(near[s].at[0, p], near_recv.at[s, 0, p])
                    each(near_copies(s, p), start)

            @pl.when(with_far)
            def _(s=s, p=p):
                arrived(far[s].at[0, p], far_recv.at[s, 0, p])
                each(far_copies(s, p), start)

            if s == 0:
                if p == 0:
                    each_head(own)
            elif p == 0:
                near_step(s - 1)
            else:
                far_step(s - 1, (s <= plane) & ((row == 1) if s == 1 else True))
        if s == 0:

            @pl.when(side == 1)
            def _():
                for p in (0, 1):
                    arrived(beside.at[p], beside_recv.at[p])
                visible = before_own(mean * rank - quarter)
                absorb_all(lambda head: jnp.concatenate([beside[p, head] for p in (0, 1)]), visible)

        far_step(s, (s == plane) & ((row == 1) if s == 0 else True))

    alive = lax.broadcasted_iota(jnp.int32, (slots, HEAD_DIM), 0) < own_count

    def write(head):
        result = (total[head] / weight_sum[head]).T
        for g in range(GROUP):
            column = pl.multiple_of((head * GROUP + g) * HEAD_DIM, HEAD_DIM)
            piece = jnp.where(alive, result[g * slots : (g + 1) * slots], 0.0)
            out_ref[:, pl.ds(column, HEAD_DIM)] = piece.astype(jnp.bfloat16)

    each_head(write)

    @pl.when(jnp.logical_not(first))
    def _():
        edge(0).wait_send()

    @pl.when(jnp.logical_not(last))
    def _():
        edge(1).wait_send()

    for p in (0, 1):
        each(own_copies(p), finish)
        for s in range(planes):
            if s < planes - 1:

                @pl.when(s < plane)
                def _(s=s, p=p):
                    each(near_copies(s, p), finish)

            @pl.when(row == 1 if s == 0 else s <= plane)
            def _(s=s, p=p):
                each(far_copies(s, p), finish)


def per_device(ranks, queries, patch_keys, patch_values, patch_counts):
    slots, width = patch_keys.shape
    quarter = slots // 6
    lanes = GROUP * slots
    planes = ranks // 4
    two_parts = (2, KV_HEADS, 2 * quarter, 2 * HEAD_DIM)
    pair = pltpu.VMEM((2, *two_parts), jnp.bfloat16)
    edges = pltpu.VMEM((2, KV_HEADS, quarter, 2 * HEAD_DIM), jnp.bfloat16)
    return pl.pallas_call(
        functools.partial(kernel, ranks),
        out_shape=jax.ShapeDtypeStruct(queries.shape, jnp.bfloat16),
        in_specs=[pl.BlockSpec(memory_space=pl.ANY)] * 4,
        out_specs=pl.BlockSpec(memory_space=pltpu.VMEM),
        scratch_shapes=[
            pltpu.SMEM(patch_counts.shape, jnp.int32),
            pltpu.VMEM((slots, width), jnp.bfloat16),
            pltpu.VMEM((slots, width), jnp.bfloat16),
            [pair] * (planes - 1),
            [pair] * planes,
            pltpu.VMEM(two_parts, jnp.bfloat16),
            pltpu.VMEM(two_parts, jnp.bfloat16),
            edges,
            edges,
            pltpu.VMEM((KV_HEADS, lanes, HEAD_DIM), jnp.bfloat16),
            pltpu.VMEM((KV_HEADS, HEAD_DIM, lanes), jnp.bfloat16),
            pltpu.VMEM((KV_HEADS, HEAD_DIM, lanes), jnp.float32),
            pltpu.VMEM((KV_HEADS, 1, lanes), jnp.float32),
            pltpu.VMEM((KV_HEADS, 1, lanes), jnp.float32),
            pltpu.SemaphoreType.DMA((3,)),
            pltpu.SemaphoreType.DMA((KV_HEADS * GROUP,)),
            pltpu.SemaphoreType.DMA((2, 3)),
            pltpu.SemaphoreType.DMA((planes, 2, 3)),
            pltpu.SemaphoreType.DMA((planes, 2)),
            pltpu.SemaphoreType.DMA((2,)),
            pltpu.SemaphoreType.DMA((planes, 2, 2)),
            pltpu.SemaphoreType.DMA((planes, 2, 2)),
            pltpu.SemaphoreType.DMA((2,)),
            pltpu.SemaphoreType.DMA((2,)),
        ],
        compiler_params=pltpu.CompilerParams(
            collective_id=0, has_side_effects=True, vmem_limit_bytes=60 * 2**20
        ),
    )(queries, patch_keys, patch_values, patch_counts)


def solution(mesh):
    placed = (
        P(("groups", "ctx"), None),
        P(("groups", "ctx"), None),
        P(("groups", "ctx"), None),
        P("groups"),
    )
    return jax.shard_map(
        functools.partial(per_device, mesh.shape["ctx"]),
        mesh=mesh,
        in_specs=placed,
        out_specs=P(("groups", "ctx"), None),
        check_vma=False,
    )
```
